32 devices in a mesh: row: 8 (over y, x, core), col: 4 (over z).
Axes of the slice: x: 2, y: 2, z: 4, core: 2. Of those that a mesh axis runs over, the one named last changes fastest.
Arguments:
- object_field: float32 [2, 4096, 2048], P(None, 'row', 'col'), may hold values from -6 to 6
- illumination: float32 [2, 256, 256], replicated, may hold values from -6 to 6
- amplitude: bfloat16 [512, 256, 256], P(('row', 'col')), may hold values from 0 to 2
- offsets: int32 [512, 2], P(('row', 'col')), may hold values from 0 to 3840, as said below
- slot_counts: int32 [32], replicated, may hold values from 1 to 16, 256 in all
Outputs:
- object_gradient: float32 [2, 4096, 2048], P(None, 'row', 'col')
- probe_gradient: float32 [2, 256, 256], replicated
The draws below stay inside these ranges and needn't reach their ends.
Inputs may be any that keep to these rules, and one draw needn't show every extreme that they name: `offsets`: slot j belongs to region d = j // 16, with row index d // 4 and column index d mod 4 (region (r, c)); its row offset lies in [r * 512, (r + 1) * 512) and its column offset in [c * 512, (c + 1) * 512), and every patch lies inside the object. Region d's live slots are its first slot_counts[d]; all counts sum to 256 and some region is full.
All inputs are finite; a program needn't handle non-finite values.
Results may differ from the reference program's by a relative error of at most 0.0045.
Values sent between devices are 32-bit elements; how exact they have to be, the bound alone decides.
No kernel may reach another device: no remote copies, remote signals or barrier semaphores. Data moves between devices by JAX's collectives and lax.ppermute only.
A program may use at most 128 MiB of HBM per device.

```python
import math
import jax
import jax.numpy as jnp
import numpy as np
from jax import lax

W = 256
TR = 512
TC = 512
CAP = 16
ROWS_OBJ = 4096
COLS_OBJ = 2048
SLOTS = 512
TOTAL = 256
DEVICES = 32


def draw_offsets(key, part):
    col_tiles = COLS_OBJ // TC
    row_tiles = ROWS_OBJ // TR
    slot_ids = jnp.arange(SLOTS, dtype=jnp.int32)
    region = slot_ids // CAP
    row_tile = region // col_tiles
    col_tile = region % col_tiles
    row_high = jnp.where(row_tile == row_tiles - 1, TR - W + 1, TR).astype(jnp.int32)
    col_high = jnp.where(col_tile == col_tiles - 1, TC - W + 1, TC).astype(jnp.int32)
    first_key, second_key = jax.random.split(key)
    row_part = jax.random.randint(first_key, (SLOTS,), 0, row_high, dtype=jnp.int32)
    col_part = jax.random.randint(second_key, (SLOTS,), 0, col_high, dtype=jnp.int32)
    first_slot = slot_ids == 0
    last_slot = slot_ids == SLOTS - CAP
    row_part = jnp.where(first_slot, 0, jnp.where(last_slot, TR - W, row_part)).astype(jnp.int32)
    col_part = jnp.where(first_slot, 0, jnp.where(last_slot, TC - W, col_part)).astype(jnp.int32)
    return jnp.stack([row_tile * TR + row_part, col_tile * TC + col_part], axis=1).astype(jnp.int32)


def level_of(rng, extent, pieces, low, high):
    def one(position, shards_of):
        draws = jax.random.uniform(jax.random.fold_in(jax.random.fold_in(rng, 6), position), (shards_of,), jnp.float32, low / len(pieces), high / len(pieces))
        return jnp.repeat(jnp.exp(draws), extent[position] // shards_of).reshape((-1,) + (1,) * (len(extent) - position - 1))

    level = one(*pieces[0])
    for cut in pieces[1:]:
        level = level * one(*cut)
    return level


def profile(amount, total, limit, slope):
    weights = [(1 << 20) // math.isqrt(standing ** slope) + 1 for standing in range(2, amount + 1)]
    spare, counts = total - limit - (amount - 1), [1] * (amount - 1)
    while spare > 0:
        candidates = [i for i in range(amount - 1) if counts[i] < limit]
        whole, remaining = sum([weights[i] for i in candidates]), spare
        for i in candidates:
            addition = min(limit - counts[i], max(1, remaining * weights[i] // whole), spare)
            counts[i] = counts[i] + addition
            spare = spare - addition
    return np.array([limit] + counts)


def uneven_parts(rng, count, total, reach, slope):
    if count == 2:
        one = jax.random.randint(rng, (), max(1, total - reach), min(reach, total - 1) + 1)
        return jnp.stack([one, total - one])
    tallies = jnp.asarray(profile(count, total, reach, slope), jnp.int32)
    couples = (count - 1) // 2
    giver, taker = tallies[1:1 + 2 * couples:2], tallies[2:2 + 2 * couples:2]
    slack = jnp.minimum(giver - 1, reach - taker)
    moved = jax.random.randint(jax.random.fold_in(rng, 1), (couples,), 0, 1 << 20) % (slack + 1)
    tallies = tallies.at[1:1 + 2 * couples:2].set(giver - moved).at[2:2 + 2 * couples:2].set(taker + moved)
    return tallies[jax.random.permutation(jax.random.fold_in(rng, 2), count)]


def noise(stream_key, dims, deviation, reach, cuts=(), kind=jnp.bfloat16):
    gain = level_of(stream_key, dims, cuts, -0.22, 0.18) if cuts else 1.0
    array = jax.random.normal(stream_key, dims, jnp.float32) * deviation * gain
    return jnp.minimum(jnp.maximum(array, -reach), reach).astype(kind)


def setup_inputs(seed: int = 0) -> dict:
    arg_keys = jax.random.split(jax.random.key(seed), 6)
    return {
        "object_field": noise(arg_keys[0], (2, ROWS_OBJ, COLS_OBJ), 1.0, 6.0, ((1, 8), (2, 4)), jnp.float32),
        "illumination": noise(arg_keys[1], (2, W, W), 1.0, 6.0, (), jnp.float32),
        "amplitude": jnp.clip(2.0 * jax.random.uniform(arg_keys[2], (SLOTS, W, W), jnp.float32) ** level_of(arg_keys[2], (SLOTS, W, W), ((0, 32),), -0.2, 0.2), 0.0, 2.0).astype(jnp.bfloat16),
        "offsets": draw_offsets(jax.random.fold_in(arg_keys[5], 71), 0),
        "slot_counts": uneven_parts(arg_keys[4], DEVICES, TOTAL, CAP, 2).astype(jnp.int32),
    }


def dft_tables(direction):
    positions = jnp.arange(W, dtype=jnp.int32)
    product = positions[:, None] * positions[None, :] % W
    angle = product.astype(jnp.float32) * (2.0 * math.pi / W)
    factor = 1.0 / math.sqrt(W)
    cosine = jnp.cos(angle) * factor
    sine = direction * jnp.sin(angle) * factor
    left = jnp.stack([jnp.stack([cosine, -sine]), jnp.stack([sine, cosine])]).astype(jnp.bfloat16)
    right = jnp.stack([jnp.stack([cosine, sine]), jnp.stack([-sine, cosine])]).astype(jnp.bfloat16)
    return (left, right)

def transform(field, tables):
    left, right = tables
    half = jnp.einsum('oiab,nibd->noad', left.astype(jnp.float32), field.astype(jnp.float32)).astype(jnp.bfloat16)
    return jnp.einsum('niab,iobd->noad', half.astype(jnp.float32), right.astype(jnp.float32))

def gradient_block(patches, amplitudes, illumination, forward, inverse):
    real_probe = illumination[0]
    imag_probe = illumination[1]
    exit_real = real_probe * patches[:, 0] - imag_probe * patches[:, 1]
    exit_imag = real_probe * patches[:, 1] + imag_probe * patches[:, 0]
    exit_wave = jnp.stack([exit_real, exit_imag], axis=1).astype(jnp.bfloat16)
    far_field = transform(exit_wave, forward)
    magnitude = jnp.sqrt(far_field[:, 0] ** 2 + far_field[:, 1] ** 2 + 0.25)
    factor = 1.0 - amplitudes.astype(jnp.float32) / magnitude
    residual = (far_field * factor[:, None]).astype(jnp.bfloat16)
    back_field = transform(residual, inverse)
    object_terms = jnp.stack([real_probe * back_field[:, 0] + imag_probe * back_field[:, 1], real_probe * back_field[:, 1] - imag_probe * back_field[:, 0]], axis=1)
    probe_terms = jnp.stack([patches[:, 0] * back_field[:, 0] + patches[:, 1] * back_field[:, 1], patches[:, 0] * back_field[:, 1] - patches[:, 1] * back_field[:, 0]], axis=1)
    return (object_terms, probe_terms)

def reference(object_field, illumination, amplitude, offsets, slot_counts):
    forward = dft_tables(-1.0)
    inverse = dft_tables(1.0)
    regions = SLOTS // CAP
    zero_index = jnp.zeros((), jnp.int32)

    def region_step(state_pair, region):
        gradient, probe_total = state_pair
        start = (region * CAP).astype(jnp.int32)
        slot_offsets = lax.dynamic_slice_in_dim(offsets, start, CAP, 0)
        slot_amplitude = lax.dynamic_slice_in_dim(amplitude, start, CAP, 0)
        patches = jax.vmap(lambda corner: lax.dynamic_slice(object_field, (zero_index, corner[0].astype(jnp.int32), corner[1].astype(jnp.int32)), (2, W, W)))(slot_offsets)
        live_mask = (jnp.arange(CAP, dtype=jnp.int32) < slot_counts[region]).astype(jnp.float32)
        object_terms, probe_terms = gradient_block(patches, slot_amplitude, illumination, forward, inverse)
        object_terms = object_terms * live_mask[:, None, None, None]
        probe_total = probe_total + lax.optimization_barrier(jnp.sum(probe_terms * live_mask[:, None, None, None], axis=0))

        def add_patch(slot_index, current):
            corner_row = slot_offsets[slot_index, 0].astype(jnp.int32)
            corner_col = slot_offsets[slot_index, 1].astype(jnp.int32)
            block = lax.dynamic_slice(current, (zero_index, corner_row, corner_col), (2, W, W))
            return lax.dynamic_update_slice(current, block + object_terms[slot_index], (zero_index, corner_row, corner_col))
        gradient = lax.fori_loop(0, CAP, add_patch, gradient)
        return ((gradient, probe_total), None)
    start_state = (jnp.zeros(object_field.shape, jnp.float32), jnp.zeros((2, W, W), jnp.float32))
    final_state, unused = lax.scan(region_step, start_state, jnp.arange(regions, dtype=jnp.int32))
    gradient, probe_total = final_state
    return (gradient, probe_total * (1.0 / math.sqrt(TOTAL)))
```

```python
import functools
import math

import jax
import jax.numpy as jnp
import numpy as np
from jax import lax
from jax.experimental import pallas as pl
from jax.experimental.pallas import tpu as pltpu
from jax.sharding import PartitionSpec as P

LANE = 128
CHUNK = 32
F32 = jnp.float32
BF16 = jnp.bfloat16


def shifted(value, axis, steps):
    count = lax.axis_size(axis)
    leading, last = (max(0, -steps), min(count, count - steps))
    return lax.ppermute(value, axis, [(source, source + steps) for source in range(leading, last)])


def dft_blocks(window):
    index = np.arange(window)
    angle = (index[:, None] * index[None, :] % window) * (2.0 * math.pi / window)
    cosine = np.cos(angle) / math.sqrt(window)
    sine = np.sin(angle) / math.sqrt(window)
    forward = np.block([[cosine, sine], [-sine, cosine]])
    inverse = np.block([[cosine, -sine], [sine, cosine]])
    return forward.astype(BF16), inverse.astype(BF16)


def slot_steps(window, tiles_count, class_low, class_high, tile_cols, columns, refs):
    (offs, counts, amplitude, forward, inverse, probe, ext, acc, pacc) = refs["io"]
    (chosen, amp, patch, ext_wave, half, resid, back_half, amp_sem) = refs["scratch"]
    slots = offs.shape[0]
    live = counts[lax.axis_index("row") * columns + lax.axis_index("col")]
    tile_rows = refs["tile_rows"]

    def first_tile(col):
        return lax.div(jnp.maximum(col - 1, 0), LANE)

    def pick(j, n):
        tile = first_tile(lax.rem(offs[j, 1], tile_cols))
        chosen[n] = j
        take = (j < live) & (tile >= class_low) & (tile < class_high)
        return n + take.astype(jnp.int32)

    total = lax.fori_loop(0, slots, pick, jnp.int32(0))

    def fetch(i):
        buffer = lax.rem(i, 2)
        return pltpu.make_async_copy(amplitude.at[chosen[i]], amp.at[buffer], amp_sem.at[buffer])

    @pl.when(total > 0)
    def _():
        fetch(0).start()

    refs["ready"]()
    lane = lax.broadcasted_iota(jnp.int32, (CHUNK, LANE), 1)

    def body(i, carry):
        @pl.when(i + 1 < total)
        def _():
            fetch(i + 1).start()

        j = chosen[i]
        row = lax.rem(offs[j, 0], tile_rows)
        col = lax.rem(offs[j, 1], tile_cols)
        tile = first_tile(col)
        rest = col - tile * LANE
        tile = tile - class_low
        turn = lax.rem(LANE - rest, LANE)
        head = lane < LANE - rest
        for base in range(0, window, CHUNK):
            rows = pl.ds(row + base, CHUNK)
            here = slice(base, base + CHUNK)
            planes = []
            for plane in range(2):
                turned = [
                    pltpu.roll(ext[plane, tile + k, rows, :], turn, 1) for k in range(3)
                ]
                planes.append(
                    [jnp.where(head, turned[k], turned[k + 1]) for k in range(2)]
                )
            for k in range(2):
                cols = slice(k * LANE, (k + 1) * LANE)
                real, imag = planes[0][k], planes[1][k]
                patch[0, here, cols] = real
                patch[1, here, cols] = imag
                probe_real, probe_imag = probe[0, here, cols], probe[1, here, cols]
                ext_wave[base : base + CHUNK, cols] = (
                    probe_real * real - probe_imag * imag
                ).astype(BF16)
                ext_wave[window + base : window + base + CHUNK, cols] = (
                    probe_real * imag + probe_imag * real
                ).astype(BF16)
        mid = jnp.dot(forward[...], ext_wave[...], preferred_element_type=F32).astype(BF16)
        half[:, :window] = mid[:window]
        half[:, window:] = mid[window:]
        far = jnp.dot(half[...], inverse[...], preferred_element_type=F32)
        fetch(i).wait()
        buffer = lax.rem(i, 2)
        for base in range(0, window, CHUNK):
            here = slice(base, base + CHUNK)
            real, imag = far[here, :window], far[here, window:]
            level = amp[buffer, here, :].astype(F32)
            factor = 1.0 - level * lax.rsqrt(real * real + imag * imag + 0.25)
            resid[here, :] = (real * factor).astype(BF16)
            resid[window + base : window + base + CHUNK, :] = (imag * factor).astype(BF16)
        mid = jnp.dot(inverse[...], resid[...], preferred_element_type=F32).astype(BF16)
        back_half[:, :window] = mid[:window]
        back_half[:, window:] = mid[window:]
        back = jnp.dot(back_half[...], forward[...], preferred_element_type=F32)
        tail = lane >= rest
        for base in range(0, window, CHUNK):
            rows = pl.ds(row + base, CHUNK)
            here = slice(base, base + CHUNK)
            terms = [[], []]
            for k in range(2):
                cols = slice(k * LANE, (k + 1) * LANE)
                real = back[here, k * LANE : (k + 1) * LANE]
                imag = back[here, window + k * LANE : window + (k + 1) * LANE]
                probe_real, probe_imag = probe[0, here, cols], probe[1, here, cols]
                patch_real, patch_imag = patch[0, here, cols], patch[1, here, cols]
                pacc[0, here, cols] += patch_real * real + patch_imag * imag
                pacc[1, here, cols] += patch_real * imag - patch_imag * real
                terms[0].append(pltpu.roll(probe_real * real + probe_imag * imag, lax.rem(rest, LANE), 1))
                terms[1].append(pltpu.roll(probe_real * imag - probe_imag * real, lax.rem(rest, LANE), 1))
            for plane in range(2):
                first, second = terms[plane]
                acc[plane, tile, rows, :] += jnp.where(tail, first, 0.0)
                acc[plane, tile + 1, rows, :] += jnp.where(tail, second, first)
                acc[plane, tile + 2, rows, :] += jnp.where(tail, 0.0, second)
        return carry

    lax.fori_loop(0, total, body, 0)


def run_copies(copies):
    for copy in copies:
        copy.start()
    return copies


def make_scratch(window, tiles, rows, copies):
    return [
        pltpu.VMEM((2, tiles, rows, LANE), F32),
        pltpu.VMEM((2, tiles, rows, LANE), F32),
        pltpu.VMEM((2, window, window), F32),
        pltpu.SMEM((32,), jnp.int32),
        pltpu.VMEM((2, window, window), BF16),
        pltpu.VMEM((2, window, window), F32),
        pltpu.VMEM((2 * window, window), BF16),
        pltpu.VMEM((window, 2 * window), BF16),
        pltpu.VMEM((2 * window, window), BF16),
        pltpu.VMEM((window, 2 * window), BF16),
        pltpu.SemaphoreType.DMA((2,)),
        pltpu.SemaphoreType.DMA((copies,)),
    ]


SMEM = pl.BlockSpec(memory_space=pltpu.SMEM)
VMEM = pl.BlockSpec(memory_space=pltpu.VMEM)
HBM = pl.BlockSpec(memory_space=pl.ANY)


def span(tile, count=1):
    return pl.ds(tile * LANE, count * LANE)


def inner_kernel(
    shape, offs, counts, amplitude, forward, inverse, probe, tile_in, lower_in,
    own, strip, spill, probe_sum,
    ext, acc, pacc, chosen, amp, patch, ext_wave, half, resid, back_half, amp_sem, sems,
):
    rows, cols, window, columns = shape
    tiles = cols // LANE
    copies = []
    for k in range(tiles):
        copies.append(pltpu.make_async_copy(
            tile_in.at[:, :, span(k)], ext.at[:, k, pl.ds(0, rows), :], sems.at[2 * k]))
        copies.append(pltpu.make_async_copy(
            lower_in.at[:, :, span(k)], ext.at[:, k, pl.ds(rows, window), :], sems.at[2 * k + 1]))
    run_copies(copies)
    acc[...] = jnp.zeros_like(acc)
    pacc[...] = jnp.zeros_like(pacc)

    def ready():
        for copy in copies:
            copy.wait()

    slot_steps(window, tiles, 0, tiles - 2, cols, columns, dict(
        io=(offs, counts, amplitude, forward, inverse, probe, ext, acc, pacc),
        scratch=(chosen, amp, patch, ext_wave, half, resid, back_half, amp_sem),
        tile_rows=rows, ready=ready))
    out = []
    for k in range(tiles - 2):
        out.append(pltpu.make_async_copy(
            acc.at[:, k, pl.ds(0, rows), :], own.at[:, :, span(k)], sems.at[2 * k]))
        out.append(pltpu.make_async_copy(
            acc.at[:, k, pl.ds(rows, window), :], strip.at[:, :, span(k)], sems.at[2 * k + 1]))
    out.append(pltpu.make_async_copy(acc.at[:, pl.ds(tiles - 2, 2)], spill, sems.at[2 * tiles]))
    out.append(pltpu.make_async_copy(pacc, probe_sum, sems.at[2 * tiles + 1]))
    run_copies(out)
    for copy in out:
        copy.wait()


def near_kernel(
    shape, offs, counts, amplitude, forward, inverse, probe, tile_in, lower_in, right_in, corner_in,
    spill_in, probe_in, own_in, strip_in,
    own, strip, spill, probe_sum,
    ext, acc, pacc, chosen, amp, patch, ext_wave, half, resid, back_half, amp_sem, sems,
):
    rows, cols, window, columns = shape
    last = cols // LANE
    copies = [
        pltpu.make_async_copy(spill_in, acc.at[:, pl.ds(0, 2)], sems.at[0]),
        pltpu.make_async_copy(probe_in, pacc, sems.at[1]),
        pltpu.make_async_copy(right_in, ext.at[:, 2, pl.ds(0, rows), :], sems.at[2]),
        pltpu.make_async_copy(corner_in, ext.at[:, 2, pl.ds(rows, window), :], sems.at[3]),
    ]
    for k in range(2):
        copies.append(pltpu.make_async_copy(
            tile_in.at[:, :, span(last - 2 + k)], ext.at[:, k, pl.ds(0, rows), :], sems.at[4 + 2 * k]))
        copies.append(pltpu.make_async_copy(
            lower_in.at[:, :, span(last - 2 + k)], ext.at[:, k, pl.ds(rows, window), :], sems.at[5 + 2 * k]))
    run_copies(copies)
    acc[:, 2] = jnp.zeros_like(acc[:, 2])

    def ready():
        for copy in copies:
            copy.wait()

    slot_steps(window, 3, last - 2, last - 1, cols, columns, dict(
        io=(offs, counts, amplitude, forward, inverse, probe, ext, acc, pacc),
        scratch=(chosen, amp, patch, ext_wave, half, resid, back_half, amp_sem),
        tile_rows=rows, ready=ready))
    out = [
        pltpu.make_async_copy(acc.at[:, 0, pl.ds(0, rows), :], own.at[:, :, span(last - 2)], sems.at[0]),
        pltpu.make_async_copy(acc.at[:, 0, pl.ds(rows, window), :], strip.at[:, :, span(last - 2)], sems.at[1]),
        pltpu.make_async_copy(acc.at[:, pl.ds(1, 2)], spill, sems.at[2]),
        pltpu.make_async_copy(pacc, probe_sum, sems.at[3]),
    ]
    run_copies(out)
    for copy in out:
        copy.wait()


def far_kernel(
    shape, offs, counts, amplitude, forward, inverse, probe, tile_in, lower_in, right_in, corner_in,
    far_top, far_bottom, far_corner, spill_in, probe_in, own_in, strip_in,
    own, strip, top, bottom, corner, probe_sum,
    ext, acc, pacc, chosen, amp, patch, ext_wave, half, resid, back_half, amp_sem, sems,
):
    rows, cols, window, columns = shape
    last = cols // LANE - 1
    copies = [
        pltpu.make_async_copy(spill_in, acc.at[:, pl.ds(0, 2)], sems.at[0]),
        pltpu.make_async_copy(probe_in, pacc, sems.at[1]),
        pltpu.make_async_copy(right_in, ext.at[:, 1, pl.ds(0, rows), :], sems.at[2]),
        pltpu.make_async_copy(corner_in, ext.at[:, 1, pl.ds(rows, window), :], sems.at[3]),
        pltpu.make_async_copy(tile_in.at[:, :, span(last)], ext.at[:, 0, pl.ds(0, rows), :], sems.at[4]),
        pltpu.make_async_copy(lower_in.at[:, :, span(last)], ext.at[:, 0, pl.ds(rows, window), :], sems.at[5]),
        pltpu.make_async_copy(far_top, ext.at[:, 2, pl.ds(0, window), :], sems.at[6]),
        pltpu.make_async_copy(far_bottom, ext.at[:, 2, pl.ds(window, rows - window), :], sems.at[7]),
        pltpu.make_async_copy(far_corner, ext.at[:, 2, pl.ds(rows, window), :], sems.at[8]),
    ]
    run_copies(copies)
    acc[:, 2] = jnp.zeros_like(acc[:, 2])

    def ready():
        for copy in copies:
            copy.wait()

    slot_steps(window, 3, last, last + 1, cols, columns, dict(
        io=(offs, counts, amplitude, forward, inverse, probe, ext, acc, pacc),
        scratch=(chosen, amp, patch, ext_wave, half, resid, back_half, amp_sem),
        tile_rows=rows, ready=ready))
    out = [
        pltpu.make_async_copy(acc.at[:, 0, pl.ds(0, rows), :], own.at[:, :, span(last)], sems.at[0]),
        pltpu.make_async_copy(acc.at[:, 0, pl.ds(rows, window), :], strip.at[:, :, span(last)], sems.at[1]),
        pltpu.make_async_copy(pacc, probe_sum, sems.at[2]),
    ]
    for k in range(2):
        out.append(pltpu.make_async_copy(
            acc.at[:, 1 + k, pl.ds(0, window), :], top.at[:, :, span(k)], sems.at[3 + 3 * k]))
        out.append(pltpu.make_async_copy(
            acc.at[:, 1 + k, pl.ds(window, rows - window), :], bottom.at[:, :, span(k)], sems.at[4 + 3 * k]))
        out.append(pltpu.make_async_copy(
            acc.at[:, 1 + k, pl.ds(rows, window), :], corner.at[:, :, span(k)], sems.at[5 + 3 * k]))
    run_copies(out)
    for copy in out:
        copy.wait()


def exchange_sum(value, window):
    for axis in ("row", "col"):
        count = lax.axis_size(axis)
        step = 1
        while step < count:
            value = value + lax.ppermute(value, axis, [(k, k ^ step) for k in range(count)])
            step *= 2
    return value


def per_device(object_field, illumination, amplitude, offsets, slot_counts):
    rows, cols = object_field.shape[1:]
    window = illumination.shape[1]
    slots = offsets.shape[0]
    columns = lax.axis_size("col")
    shape = (rows, cols, window, columns)
    forward, inverse = dft_blocks(window)
    forward, inverse = jnp.asarray(forward), jnp.asarray(inverse)

    near = shifted(object_field[:, :, :LANE], "col", -1)
    lower = shifted(object_field[:, :window, :], "row", -1)
    far_top = shifted(object_field[:, :window, LANE:window], "col", -1)
    far_bottom = shifted(object_field[:, window:, LANE:window], "col", -1)
    near_corner = shifted(near[:, :window], "row", -1)
    far_corner = shifted(far_top, "row", -1)

    def sds(*dims):
        return jax.ShapeDtypeStruct(dims, F32)

    common = (offsets, slot_counts, amplitude, forward, inverse, illumination)
    common_specs = [SMEM, SMEM, HBM, VMEM, VMEM, VMEM]
    reach = rows + window
    params = pltpu.CompilerParams(vmem_limit_bytes=48 * 1024 * 1024)
    flops = 16 * 2 * window**3

    def cost(count):
        return pl.CostEstimate(flops=flops * count, bytes_accessed=8 * 2**20, transcendentals=0)

    own, strip, spill, probe_sum = pl.pallas_call(
        functools.partial(inner_kernel, shape),
        out_shape=[sds(2, rows, cols), sds(2, window, cols), sds(2, 2, reach, LANE), sds(2, window, window)],
        in_specs=common_specs + [HBM] * 2,
        out_specs=[HBM] * 4,
        scratch_shapes=make_scratch(window, cols // LANE, reach, 12),
        compiler_params=params,
        cost_estimate=cost(8),
        name="inner_slots",
    )(*common, object_field, lower)
    own, strip, spill, probe_sum = pl.pallas_call(
        functools.partial(near_kernel, shape),
        out_shape=[sds(2, rows, cols), sds(2, window, cols), sds(2, 2, reach, LANE), sds(2, window, window)],
        in_specs=common_specs + [HBM] * 8,
        out_specs=[HBM] * 4,
        input_output_aliases={12: 0, 13: 1},
        scratch_shapes=make_scratch(window, 3, reach, 12),
        compiler_params=params,
        cost_estimate=cost(4),
        name="near_slots",
    )(*common, object_field, lower, near, near_corner, spill, probe_sum, own, strip)
    own, strip, top, bottom, corner, probe_sum = pl.pallas_call(
        functools.partial(far_kernel, shape),
        out_shape=[sds(2, rows, cols), sds(2, window, cols), sds(2, window, window),
                   sds(2, rows - window, window), sds(2, window, window), sds(2, window, window)],
        in_specs=common_specs + [HBM] * 11,
        out_specs=[HBM] * 6,
        input_output_aliases={15: 0, 16: 1},
        scratch_shapes=make_scratch(window, 3, reach, 12),
        compiler_params=params,
        cost_estimate=cost(4),
        name="far_slots",
    )(*common, object_field, lower, near, near_corner, far_top, far_bottom, far_corner,
      spill, probe_sum, own, strip)

    bottom_back = shifted(bottom, "col", 1)
    corner_back = shifted(corner, "row", 1)
    strip_back = shifted(strip, "row", 1)
    top_back = shifted(top + corner_back, "col", 1)
    own = own.at[:, :window, :].add(strip_back)
    own = own.at[:, window:, :window].add(bottom_back)
    own = own.at[:, :window, :window].add(top_back)
    summed = exchange_sum(probe_sum, window)
    live_total = slots * lax.axis_size("row") * lax.axis_size("col") // 2
    return own, summed * (1.0 / math.sqrt(live_total))


def solution(mesh):
    return jax.shard_map(
        per_device,
        mesh=mesh,
        in_specs=(
            P(None, "row", "col"),
            P(),
            P(("row", "col"), None, None),
            P(("row", "col"), None),
            P(),
        ),
        out_specs=(P(None, "row", "col"), P()),
        check_vma=False,
    )
```

```python
import functools
import math

import jax
import jax.numpy as jnp
import numpy as np
from jax import lax
from jax.experimental import pallas as pl
from jax.experimental.pallas import tpu as pltpu
from jax.sharding import PartitionSpec as P

LANE = 128
CHUNK = 32
PAIR = 4
VMEM_LIMIT = 28 * 1024 * 1024
F32 = jnp.float32
BF16 = jnp.bfloat16


def shifted(value, axis, steps):
    count = lax.axis_size(axis)
    leading, last = (max(0, -steps), min(count, count - steps))
    return lax.ppermute(value, axis, [(source, source + steps) for source in range(leading, last)])


def dft_blocks(window):
    index = np.arange(window)
    angle = (index[:, None] * index[None, :] % window) * (2.0 * math.pi / window)
    cosine = np.cos(angle) / math.sqrt(window)
    sine = np.sin(angle) / math.sqrt(window)
    forward = np.block([[cosine, sine], [-sine, cosine]])
    inverse = np.block([[cosine, -sine], [sine, cosine]])
    return forward.astype(BF16), inverse.astype(BF16)


def slot_steps(window, first, member, tile_cols, columns, refs):
    (offs, counts, amplitude, *tables_in, ext, acc, pacc) = refs["io"]
    (chosen, amp, patch, ext_wave, half, resid, back_half, amp_sem, *tables, table_sem) = refs["scratch"]
    (forward, inverse, probe) = tables
    loads = run_copies([
        pltpu.make_async_copy(tables_in[k], tables[k], table_sem.at[k]) for k in range(3)])
    slots = offs.shape[0]
    live = counts[lax.axis_index("row") * columns + lax.axis_index("col")]
    tile_rows = refs["tile_rows"]

    def first_tile(col):
        return lax.div(jnp.maximum(col - 1, 0), LANE)

    def pick(j, n):
        tile = first_tile(lax.rem(offs[j, 1], tile_cols))
        chosen[n] = j
        take = (j < live) & member(lax.rem(offs[j, 0], tile_rows), tile)
        return n + take.astype(jnp.int32)

    total = lax.fori_loop(0, slots, pick, jnp.int32(0))

    def fetch(i):
        buffer = lax.rem(i, 2 * PAIR)
        return pltpu.make_async_copy(
            amplitude.at[chosen[i]], amp.at[buffer], amp_sem.at[buffer])

    def fill(n):
        chosen[n] = chosen[total - 1]

    for k in range(PAIR - 1):
        @pl.when(total > 0)
        def _():
            fill(total + k)

    groups = lax.div(total + PAIR - 1, PAIR)

    @pl.when(total > 0)
    def _():
        for k in range(PAIR):
            fetch(k).start()

    refs["ready"]()
    for load in loads:
        load.wait()
    lane = lax.broadcasted_iota(jnp.int32, (CHUNK, LANE), 1)

    def body(group, carry):
        @pl.when(group + 1 < groups)
        def _():
            for k in range(PAIR):
                fetch((group + 1) * PAIR + k).start()

        places = []
        for s in range(PAIR):
            j = chosen[group * PAIR + s]
            row = lax.rem(offs[j, 0], tile_rows)
            col = lax.rem(offs[j, 1], tile_cols)
            tile = first_tile(col)
            places.append((row, tile - first, col - tile * LANE))
        for s, (row, tile, rest) in enumerate(places):
            turn = lax.rem(LANE - rest, LANE)
            head = lane < LANE - rest
            for base in range(0, window, CHUNK):
                rows = pl.ds(row + base, CHUNK)
                here = slice(base, base + CHUNK)
                planes = []
                for plane in range(2):
                    turned = [
                        pltpu.roll(ext[plane, tile + k, rows, :], turn, 1) for k in range(3)
                    ]
                    planes.append(
                        [jnp.where(head, turned[k], turned[k + 1]) for k in range(2)]
                    )
                for k in range(2):
                    cols = slice(k * LANE, (k + 1) * LANE)
                    real, imag = planes[0][k], planes[1][k]
                    patch[s, 0, here, cols] = real
                    patch[s, 1, here, cols] = imag
                    probe_real, probe_imag = probe[0, here, cols], probe[1, here, cols]
                    ext_wave[s, base : base + CHUNK, cols] = (
                        probe_real * real - probe_imag * imag
                    ).astype(BF16)
                    ext_wave[s, window + base : window + base + CHUNK, cols] = (
                        probe_real * imag + probe_imag * real
                    ).astype(BF16)
        for s in range(PAIR):
            mid = jnp.dot(forward[...], ext_wave[s], preferred_element_type=F32).astype(BF16)
            half[s, :, :window] = mid[:window]
            half[s, :, window:] = mid[window:]
        for s in range(PAIR):
            fetch(group * PAIR + s).wait()
        for s in range(PAIR):
            far = jnp.dot(half[s], inverse[...], preferred_element_type=F32)
            buffer = lax.rem(group * PAIR + s, 2 * PAIR)
            for base in range(0, window, CHUNK):
                here = slice(base, base + CHUNK)
                real, imag = far[here, :window], far[here, window:]
                level = amp[buffer, here, :].astype(F32)
                factor = 1.0 - level * lax.rsqrt(real * real + imag * imag + 0.25)
                resid[s, here, :] = (real * factor).astype(BF16)
                resid[s, window + base : window + base + CHUNK, :] = (imag * factor).astype(BF16)
        for s in range(PAIR):
            mid = jnp.dot(inverse[...], resid[s], preferred_element_type=F32).astype(BF16)
            back_half[s, :, :window] = mid[:window]
            back_half[s, :, window:] = mid[window:]
        for s, (row, tile, rest) in enumerate(places):
            back = jnp.dot(back_half[s], forward[...], preferred_element_type=F32)
            turn = lax.rem(rest, LANE)
            tail = lane >= rest
            weight = (group * PAIR + s < total).astype(F32)
            for base in range(0, window, CHUNK):
                rows = pl.ds(row + base, CHUNK)
                here = slice(base, base + CHUNK)
                terms = [[], []]
                for k in range(2):
                    cols = slice(k * LANE, (k + 1) * LANE)
                    real = back[here, k * LANE : (k + 1) * LANE]
                    imag = back[here, window + k * LANE : window + (k + 1) * LANE]
                    if s:
                        real, imag = real * weight, imag * weight
                    probe_real, probe_imag = probe[0, here, cols], probe[1, here, cols]
                    patch_real, patch_imag = patch[s, 0, here, cols], patch[s, 1, here, cols]
                    pacc[0, here, cols] += patch_real * real + patch_imag * imag
                    pacc[1, here, cols] += patch_real * imag - patch_imag * real
                    terms[0].append(pltpu.roll(probe_real * real + probe_imag * imag, turn, 1))
                    terms[1].append(pltpu.roll(probe_real * imag - probe_imag * real, turn, 1))
                for plane in range(2):
                    left, right = terms[plane]
                    acc[plane, tile, rows, :] += jnp.where(tail, left, 0.0)
                    acc[plane, tile + 1, rows, :] += jnp.where(tail, right, left)
                    acc[plane, tile + 2, rows, :] += jnp.where(tail, 0.0, right)
        return carry

    lax.fori_loop(0, groups, body, 0)


def run_copies(copies):
    for copy in copies:
        copy.start()
    return copies


def make_scratch(window, tiles, rows, copies):
    return [
        pltpu.VMEM((2, tiles, rows, LANE), F32),
        pltpu.VMEM((2, tiles, rows, LANE), F32),
        pltpu.VMEM((2, window, window), F32),
        pltpu.SMEM((32,), jnp.int32),
        pltpu.VMEM((2 * PAIR, window, window), BF16),
        pltpu.VMEM((PAIR, 2, window, window), F32),
        pltpu.VMEM((PAIR, 2 * window, window), BF16),
        pltpu.VMEM((PAIR, window, 2 * window), BF16),
        pltpu.VMEM((PAIR, 2 * window, window), BF16),
        pltpu.VMEM((PAIR, window, 2 * window), BF16),
        pltpu.SemaphoreType.DMA((2 * PAIR,)),
        pltpu.VMEM((2 * window, 2 * window), BF16),
        pltpu.VMEM((2 * window, 2 * window), BF16),
        pltpu.VMEM((2, window, window), F32),
        pltpu.SemaphoreType.DMA((3,)),
        pltpu.SemaphoreType.DMA((copies,)),
    ]


SMEM = pl.BlockSpec(memory_space=pltpu.SMEM)
VMEM = pl.BlockSpec(memory_space=pltpu.VMEM)
HBM = pl.BlockSpec(memory_space=pl.ANY)


def span(tile, count=1):
    return pl.ds(tile * LANE, count * LANE)


def slice_kernel(spots, tile_in, *refs):
    *outs, sems = refs
    copies = run_copies([
        pltpu.make_async_copy(
            tile_in.at[:, pl.ds(row, rows), pl.ds(col, cols)], outs[k], sems.at[k])
        for k, (row, rows, col, cols) in enumerate(spots)
    ])
    for copy in copies:
        copy.wait()


def slices(tile, spots, name):
    return pl.pallas_call(
        functools.partial(slice_kernel, spots),
        out_shape=[jax.ShapeDtypeStruct((2, rows, cols), F32) for _, rows, _, cols in spots],
        in_specs=[HBM],
        out_specs=[VMEM] * len(spots),
        scratch_shapes=[pltpu.SemaphoreType.DMA((len(spots),))],
        name=name,
    )(tile)


def merge_kernel(places, own_in, *refs):
    count = len(places)
    added, (own, *held), sems = refs[:count], refs[count:-1], refs[-1]
    spots = [
        own.at[:, pl.ds(row, rows), pl.ds(col, cols)] for row, rows, col, cols in places]
    loads = []
    for k in range(count):
        loads += run_copies([
            pltpu.make_async_copy(spots[k], held[2 * k], sems.at[3 * k]),
            pltpu.make_async_copy(added[k], held[2 * k + 1], sems.at[3 * k + 1]),
        ])
    stores = []
    for k in range(count):
        loads[2 * k].wait()
        loads[2 * k + 1].wait()
        held[2 * k][...] += held[2 * k + 1][...]
        stores += run_copies([pltpu.make_async_copy(held[2 * k], spots[k], sems.at[3 * k + 2])])
    for store in stores:
        store.wait()


def merge(own, blocks, places, name):
    scratch = []
    for _, rows, _, cols in places:
        scratch += [pltpu.VMEM((2, rows, cols), F32)] * 2
    return pl.pallas_call(
        functools.partial(merge_kernel, places),
        out_shape=jax.ShapeDtypeStruct(own.shape, F32),
        in_specs=[HBM] * (1 + len(blocks)),
        out_specs=HBM,
        input_output_aliases={0: 0},
        scratch_shapes=scratch + [pltpu.SemaphoreType.DMA((3 * len(blocks),))],
        compiler_params=pltpu.CompilerParams(vmem_limit_bytes=VMEM_LIMIT),
        name=name,
    )(own, *blocks)


def slots_of(shape, first, member, io, scratch, copies):
    rows, cols, window, columns = shape

    def ready():
        for copy in copies:
            copy.wait()

    slot_steps(window, first, member, cols, columns, dict(
        io=io, scratch=scratch, tile_rows=rows, ready=ready))


def inside_kernel(
    shape, offs, counts, amplitude, forward, inverse, probe, tile_in, part, probe_sum,
    ext, acc, pacc, *scratch_sems,
):
    *scratch, sems = scratch_sems
    rows, cols, window, columns = shape
    tiles = cols // LANE
    copies = run_copies([
        pltpu.make_async_copy(tile_in.at[:, :, span(k)], ext.at[:, k], sems.at[k])
        for k in range(tiles)
    ])
    acc[...] = jnp.zeros_like(acc)
    pacc[...] = jnp.zeros_like(pacc)
    slots_of(
        shape, 0, lambda row, tile: (row <= rows - window) & (tile < tiles - 2),
        (offs, counts, amplitude, forward, inverse, probe, ext, acc, pacc), scratch, copies)
    out = run_copies([
        pltpu.make_async_copy(acc, part, sems.at[0]),
        pltpu.make_async_copy(pacc, probe_sum, sems.at[1]),
    ])
    for copy in out:
        copy.wait()


def below_kernel(
    shape, offs, counts, amplitude, forward, inverse, probe, tile_in, lower_in, part, probe_in,
    own, strip, spill, probe_sum,
    ext, acc, pacc, *scratch_sems,
):
    *scratch, sems = scratch_sems
    rows, cols, window, columns = shape
    tiles = cols // LANE
    copies = [
        pltpu.make_async_copy(part, acc.at[:, :, pl.ds(0, rows), :], sems.at[2 * tiles]),
        pltpu.make_async_copy(probe_in, pacc, sems.at[2 * tiles + 1]),
    ]
    for k in range(tiles):
        copies.append(pltpu.make_async_copy(
            tile_in.at[:, :, span(k)], ext.at[:, k, pl.ds(0, rows), :], sems.at[2 * k]))
        copies.append(pltpu.make_async_copy(
            lower_in.at[:, :, span(k)], ext.at[:, k, pl.ds(rows, window), :], sems.at[2 * k + 1]))
    run_copies(copies)
    acc[:, :, rows:, :] = jnp.zeros((2, tiles, window, LANE), F32)
    slots_of(
        shape, 0, lambda row, tile: (row > rows - window) & (tile < tiles - 2),
        (offs, counts, amplitude, forward, inverse, probe, ext, acc, pacc), scratch, copies)
    out = []
    for k in range(tiles - 2):
        out.append(pltpu.make_async_copy(
            acc.at[:, k, pl.ds(0, rows), :], own.at[:, :, span(k)], sems.at[2 * k]))
        out.append(pltpu.make_async_copy(
            acc.at[:, k, pl.ds(rows, window), :], strip.at[:, :, span(k)], sems.at[2 * k + 1]))
    out.append(pltpu.make_async_copy(acc.at[:, pl.ds(tiles - 2, 2)], spill, sems.at[2 * tiles]))
    out.append(pltpu.make_async_copy(pacc, probe_sum, sems.at[2 * tiles + 1]))
    run_copies(out)
    for copy in out:
        copy.wait()


def across_kernel(
    shape, offs, counts, amplitude, forward, inverse, probe, tile_in, lower_in, top_in, bottom_in, corner_in,
    spill, probe_in, own_in, strip_in,
    own, strip, top, bottom, corner, probe_sum,
    ext, acc, pacc, *scratch_sems,
):
    *scratch, sems = scratch_sems
    rows, cols, window, columns = shape
    first = cols // LANE - 2
    copies = [
        pltpu.make_async_copy(spill, acc.at[:, pl.ds(0, 2)], sems.at[0]),
        pltpu.make_async_copy(probe_in, pacc, sems.at[1]),
    ]
    for k in range(2):
        for n, (source, start, count) in enumerate((
            (tile_in.at[:, :, span(first + k)], 0, rows),
            (lower_in.at[:, :, span(first + k)], rows, window),
        )):
            copies.append(pltpu.make_async_copy(
                source, ext.at[:, k, pl.ds(start, count), :], sems.at[2 + 5 * k + n]))
        for n, (source, start, count) in enumerate((
            (top_in, 0, window), (bottom_in, window, rows - window), (corner_in, rows, window),
        )):
            copies.append(pltpu.make_async_copy(
                source.at[:, :, span(k)], ext.at[:, 2 + k, pl.ds(start, count), :], sems.at[4 + 5 * k + n]))
    run_copies(copies)
    acc[:, 2:] = jnp.zeros_like(acc[:, 2:])
    slots_of(
        shape, first, lambda row, tile: tile >= first,
        (offs, counts, amplitude, forward, inverse, probe, ext, acc, pacc), scratch, copies)
    out = [pltpu.make_async_copy(pacc, probe_sum, sems.at[0])]
    for k in range(2):
        for n, (target, place, start, count) in enumerate((
            (own.at[:, :, span(first + k)], k, 0, rows),
            (strip.at[:, :, span(first + k)], k, rows, window),
            (top.at[:, :, span(k)], 2 + k, 0, window),
            (bottom.at[:, :, span(k)], 2 + k, window, rows - window),
            (corner.at[:, :, span(k)], 2 + k, rows, window),
        )):
            out.append(pltpu.make_async_copy(
                acc.at[:, place, pl.ds(start, count), :], target, sems.at[1 + 5 * k + n]))
    run_copies(out)
    for copy in out:
        copy.wait()


def exchange_total(value, axis):
    count = lax.axis_size(axis)
    step = 1
    while step < count:
        masks = (1, 2, 3) if 4 * step <= count else (1,)
        terms = [value] + [
            lax.ppermute(value, axis, [(k, k ^ (mask * step)) for k in range(count)]) for mask in masks
        ]
        while len(terms) > 1:
            terms = [terms[k] + terms[k + 1] for k in range(0, len(terms), 2)]
        value = terms[0]
        step *= len(masks) + 1
    return value


def per_device(object_field, illumination, amplitude, offsets, slot_counts):
    rows, cols = object_field.shape[1:]
    window = illumination.shape[1]
    slots = offsets.shape[0]
    columns = lax.axis_size("col")
    shape = (rows, cols, window, columns)
    tiles = cols // LANE
    reach = rows + window
    forward, inverse = dft_blocks(window)
    forward, inverse = jnp.asarray(forward), jnp.asarray(inverse)
    params = pltpu.CompilerParams(vmem_limit_bytes=VMEM_LIMIT)

    def sds(*dims):
        return jax.ShapeDtypeStruct(dims, F32)

    def slots_call(kernel, count, outs, extra, place, tiles_held, aliases=None):
        return pl.pallas_call(
            functools.partial(kernel, shape),
            out_shape=[sds(*dims) for dims in outs],
            in_specs=[SMEM, SMEM] + [HBM] * (4 + len(extra)),
            out_specs=[HBM] * len(outs),
            input_output_aliases=aliases or {},
            scratch_shapes=make_scratch(window, tiles_held, place, 12),
            compiler_params=params,
            cost_estimate=pl.CostEstimate(
                flops=32 * window**3 * count, bytes_accessed=8 * 2**20, transcendentals=0),
            name=kernel.__name__,
        )(offsets, slot_counts, amplitude, forward, inverse, illumination, *extra)

    plane = (2, window, window)
    (top_own,) = slices(object_field, ((0, window, 0, window),), "slice_top")
    tile, top_own = lax.optimization_barrier((object_field, top_own))
    bottom_own, lower_own = slices(
        tile, ((window, rows - window, 0, window), (0, window, 0, cols)), "slice_rest")
    top_right = shifted(top_own, "col", -1)
    lower = shifted(lower_own, "row", -1)
    bottom_right = shifted(bottom_own, "col", -1)
    part, probe_sum = slots_call(
        inside_kernel, 8, [(2, tiles, rows, LANE), plane], (object_field,), rows, tiles)
    top_right, part = lax.optimization_barrier((top_right, part))
    corner_right = shifted(top_right, "row", -1)
    own, strip, spill, probe_sum = slots_call(
        below_kernel, 8, [(2, rows, cols), (2, window, cols), (2, 2, reach, LANE), plane],
        (object_field, lower, part, probe_sum), reach, tiles)
    own, strip, top, bottom, corner, probe_sum = slots_call(
        across_kernel, 8,
        [(2, rows, cols), (2, window, cols), plane, (2, rows - window, window), plane, plane],
        (object_field, lower, top_right, bottom_right, corner_right, spill, probe_sum, own, strip),
        reach, 4, {13: 0, 14: 1})

    corner_back = shifted(corner, "row", 1)
    bottom_back = shifted(bottom, "col", 1)
    pieces = lax.axis_size("row")
    scattered = lax.all_to_all(
        probe_sum.reshape(pieces, -1, window), "row", 0, 0, tiled=True)
    scattered, corner_back, bottom_back, strip = lax.optimization_barrier(
        (scattered, corner_back, bottom_back, strip))
    top_back = shifted(top + corner_back, "col", 1)
    strip_back = shifted(strip, "row", 1)
    piece = exchange_total(jnp.sum(scattered, axis=0), "col")
    summed = lax.all_gather(piece, "row").reshape(plane)
    own = merge(own, (strip_back, bottom_back),
                ((0, window, 0, cols), (window, rows - window, 0, window)), "first_merge")
    own = merge(own, (top_back,), ((0, window, 0, window),), "last_merge")
    live_total = slots * lax.axis_size("row") * lax.axis_size("col") // 2
    return own, summed * (1.0 / math.sqrt(live_total))


def solution(mesh):
    return jax.shard_map(
        per_device,
        mesh=mesh,
        in_specs=(
            P(None, "row", "col"),
            P(),
            P(("row", "col"), None, None),
            P(("row", "col"), None),
            P(),
        ),
        out_specs=(P(None, "row", "col"), P()),
        check_vma=False,
    )
```

```python
import functools
import math

import jax
import jax.numpy as jnp
import numpy as np
from jax import lax
from jax.experimental import pallas as pl
from jax.experimental.pallas import tpu as pltpu
from jax.sharding import PartitionSpec as P

LANE = 128
CHUNK = 32
PAIR = 4
VMEM_LIMIT = 28 * 1024 * 1024
F32 = jnp.float32
BF16 = jnp.bfloat16


def shifted(value, axis, steps):
    count = lax.axis_size(axis)
    leading, last = (max(0, -steps), min(count, count - steps))
    return lax.ppermute(value, axis, [(source, source + steps) for source in range(leading, last)])


def dft_blocks(window):
    index = np.arange(window)
    angle = (index[:, None] * index[None, :] % window) * (2.0 * math.pi / window)
    cosine = np.cos(angle) / math.sqrt(window)
    sine = np.sin(angle) / math.sqrt(window)
    forward = np.block([[cosine, sine], [-sine, cosine]])
    inverse = np.block([[cosine, -sine], [sine, cosine]])
    return forward.astype(BF16), inverse.astype(BF16)


def slot_steps(window, first, member, tile_cols, columns, refs):
    (offs, counts, amplitude, *tables_in, ext, acc, pacc) = refs["io"]
    (chosen, amp, patch, ext_wave, half, resid, back_half, amp_sem, *tables, table_sem) = refs["scratch"]
    (forward, inverse, probe) = tables
    loads = run_copies([
        pltpu.make_async_copy(tables_in[k], tables[k], table_sem.at[k]) for k in range(3)])
    slots = offs.shape[0]
    live = counts[lax.axis_index("row") * columns + lax.axis_index("col")]
    tile_rows = refs["tile_rows"]

    def first_tile(col):
        return lax.div(jnp.maximum(col - 1, 0), LANE)

    def pick(j, n):
        tile = first_tile(lax.rem(offs[j, 1], tile_cols))
        chosen[n] = j
        take = (j < live) & member(lax.rem(offs[j, 0], tile_rows), tile)
        return n + take.astype(jnp.int32)

    total = lax.fori_loop(0, slots, pick, jnp.int32(0))

    def fetch(i):
        buffer = lax.rem(i, 2 * PAIR)
        return pltpu.make_async_copy(
            amplitude.at[chosen[i]], amp.at[buffer], amp_sem.at[buffer])

    whole = lax.div(total, PAIR)
    left_over = total - whole * PAIR
    half_group = (left_over > 0) & (left_over <= PAIR // 2)
    full_groups = whole + (left_over > PAIR // 2).astype(jnp.int32)
    padded = full_groups * PAIR + half_group.astype(jnp.int32) * (PAIR // 2)

    for k in range(PAIR - 1):
        @pl.when(total > 0)
        def _():
            chosen[total + k] = chosen[total - 1]

    def fetch_from(base):
        for k in range(PAIR):
            @pl.when(base + k < padded)
            def _():
                fetch(base + k).start()

    fetch_from(0)

    refs["ready"]()
    for load in loads:
        load.wait()
    lane = lax.broadcasted_iota(jnp.int32, (CHUNK, LANE), 1)

    def body(base, size):
        fetch_from(base + size)
        places = []
        for s in range(size):
            j = chosen[base + s]
            row = lax.rem(offs[j, 0], tile_rows)
            col = lax.rem(offs[j, 1], tile_cols)
            tile = first_tile(col)
            places.append((row, tile - first, col - tile * LANE))
        def extract(s):
            row, tile, rest = places[s]
            turn = lax.rem(LANE - rest, LANE)
            head = lane < LANE - rest
            for line in range(0, window, CHUNK):
                rows = pl.ds(row + line, CHUNK)
                here = slice(line, line + CHUNK)
                planes = []
                for plane in range(2):
                    turned = [
                        pltpu.roll(ext[plane, tile + k, rows, :], turn, 1) for k in range(3)
                    ]
                    planes.append(
                        [jnp.where(head, turned[k], turned[k + 1]) for k in range(2)]
                    )
                for k in range(2):
                    cols = slice(k * LANE, (k + 1) * LANE)
                    real, imag = planes[0][k], planes[1][k]
                    patch[s, 0, here, cols] = real
                    patch[s, 1, here, cols] = imag
                    probe_real, probe_imag = probe[0, here, cols], probe[1, here, cols]
                    ext_wave[s, line : line + CHUNK, cols] = (
                        probe_real * real - probe_imag * imag
                    ).astype(BF16)
                    ext_wave[s, window + line : window + line + CHUNK, cols] = (
                        probe_real * imag + probe_imag * real
                    ).astype(BF16)
                yield

        def rows_forward(s):
            for n in range(2):
                part = slice(n * window, (n + 1) * window)
                half[s, :, part] = jnp.dot(
                    forward[part, :], ext_wave[s], preferred_element_type=F32).astype(BF16)
                yield

        def columns_forward(s):
            far = jnp.dot(half[s], inverse[...], preferred_element_type=F32)
            yield
            buffer = lax.rem(base + s, 2 * PAIR)
            for line in range(0, window, CHUNK):
                here = slice(line, line + CHUNK)
                real, imag = far[here, :window], far[here, window:]
                level = amp[buffer, here, :].astype(F32)
                factor = 1.0 - level * lax.rsqrt(real * real + imag * imag + 0.25)
                resid[s, here, :] = (real * factor).astype(BF16)
                resid[s, window + line : window + line + CHUNK, :] = (imag * factor).astype(BF16)
                yield

        def rows_back(s):
            for n in range(2):
                part = slice(n * window, (n + 1) * window)
                back_half[s, :, part] = jnp.dot(
                    inverse[part, :], resid[s], preferred_element_type=F32).astype(BF16)
                yield

        def columns_back(s):
            row, tile, rest = places[s]
            back = jnp.dot(back_half[s], forward[...], preferred_element_type=F32)
            yield
            turn = lax.rem(rest, LANE)
            tail = lane >= rest
            weight = (base + s < total).astype(F32)
            for line in range(0, window, CHUNK):
                rows = pl.ds(row + line, CHUNK)
                here = slice(line, line + CHUNK)
                terms = [[], []]
                for k in range(2):
                    cols = slice(k * LANE, (k + 1) * LANE)
                    real = back[here, k * LANE : (k + 1) * LANE]
                    imag = back[here, window + k * LANE : window + (k + 1) * LANE]
                    if s:
                        real, imag = real * weight, imag * weight
                    probe_real, probe_imag = probe[0, here, cols], probe[1, here, cols]
                    patch_real, patch_imag = patch[s, 0, here, cols], patch[s, 1, here, cols]
                    pacc[0, here, cols] += patch_real * real + patch_imag * imag
                    pacc[1, here, cols] += patch_real * imag - patch_imag * real
                    terms[0].append(pltpu.roll(probe_real * real + probe_imag * imag, turn, 1))
                    terms[1].append(pltpu.roll(probe_real * imag - probe_imag * real, turn, 1))
                for plane in range(2):
                    left, right = terms[plane]
                    acc[plane, tile, rows, :] += jnp.where(tail, left, 0.0)
                    acc[plane, tile + 1, rows, :] += jnp.where(tail, right, left)
                    acc[plane, tile + 2, rows, :] += jnp.where(tail, 0.0, right)
                yield

        for s in range(size):
            fetch(base + s).wait()
        stages = (extract, rows_forward, columns_forward, rows_back, columns_back)
        for step in range(size + len(stages) - 1):
            running = [
                stages[step - s](s) for s in reversed(range(size)) if 0 <= step - s < len(stages)]
            for work in running:
                for _ in work:
                    pass

    def full(group, carry):
        body(group * PAIR, PAIR)
        return carry

    lax.fori_loop(0, full_groups, full, 0)

    @pl.when(half_group)
    def _():
        body(full_groups * PAIR, PAIR // 2)


def run_copies(copies):
    for copy in copies:
        copy.start()
    return copies


def make_scratch(window, tiles, rows, copies):
    return [
        pltpu.VMEM((2, tiles, rows, LANE), F32),
        pltpu.VMEM((2, tiles, rows, LANE), F32),
        pltpu.VMEM((2, window, window), F32),
        pltpu.SMEM((32,), jnp.int32),
        pltpu.VMEM((2 * PAIR, window, window), BF16),
        pltpu.VMEM((PAIR, 2, window, window), F32),
        pltpu.VMEM((PAIR, 2 * window, window), BF16),
        pltpu.VMEM((PAIR, window, 2 * window), BF16),
        pltpu.VMEM((PAIR, 2 * window, window), BF16),
        pltpu.VMEM((PAIR, window, 2 * window), BF16),
        pltpu.SemaphoreType.DMA((2 * PAIR,)),
        pltpu.VMEM((2 * window, 2 * window), BF16),
        pltpu.VMEM((2 * window, 2 * window), BF16),
        pltpu.VMEM((2, window, window), F32),
        pltpu.SemaphoreType.DMA((3,)),
        pltpu.SemaphoreType.DMA((copies,)),
    ]


SMEM = pl.BlockSpec(memory_space=pltpu.SMEM)
VMEM = pl.BlockSpec(memory_space=pltpu.VMEM)
HBM = pl.BlockSpec(memory_space=pl.ANY)


def span(tile, count=1):
    return pl.ds(tile * LANE, count * LANE)


def slice_kernel(spots, tile_in, *refs):
    *outs, sems = refs
    copies = run_copies([
        pltpu.make_async_copy(
            tile_in.at[:, pl.ds(row, rows), pl.ds(col, cols)], outs[k], sems.at[k])
        for k, (row, rows, col, cols) in enumerate(spots)
    ])
    for copy in copies:
        copy.wait()


def slices(tile, spots, name):
    return pl.pallas_call(
        functools.partial(slice_kernel, spots),
        out_shape=[jax.ShapeDtypeStruct((2, rows, cols), F32) for _, rows, _, cols in spots],
        in_specs=[HBM],
        out_specs=[VMEM] * len(spots),
        scratch_shapes=[pltpu.SemaphoreType.DMA((len(spots),))],
        name=name,
    )(tile)


def merge_kernel(places, own_in, *refs):
    count = len(places)
    added, (own, *held), sems = refs[:count], refs[count:-1], refs[-1]
    spots = [
        own.at[:, pl.ds(row, rows), pl.ds(col, cols)] for row, rows, col, cols in places]
    loads = []
    for k in range(count):
        loads += run_copies([
            pltpu.make_async_copy(spots[k], held[2 * k], sems.at[3 * k]),
            pltpu.make_async_copy(added[k], held[2 * k + 1], sems.at[3 * k + 1]),
        ])
    stores = []
    for k in range(count):
        loads[2 * k].wait()
        loads[2 * k + 1].wait()
        held[2 * k][...] += held[2 * k + 1][...]
        stores += run_copies([pltpu.make_async_copy(held[2 * k], spots[k], sems.at[3 * k + 2])])
    for store in stores:
        store.wait()


def merge(own, blocks, places, name):
    scratch = []
    for _, rows, _, cols in places:
        scratch += [pltpu.VMEM((2, rows, cols), F32)] * 2
    return pl.pallas_call(
        functools.partial(merge_kernel, places),
        out_shape=jax.ShapeDtypeStruct(own.shape, F32),
        in_specs=[HBM] * (1 + len(blocks)),
        out_specs=HBM,
        input_output_aliases={0: 0},
        scratch_shapes=scratch + [pltpu.SemaphoreType.DMA((3 * len(blocks),))],
        compiler_params=pltpu.CompilerParams(vmem_limit_bytes=VMEM_LIMIT),
        name=name,
    )(own, *blocks)


def slots_of(shape, first, member, io, scratch, copies):
    rows, cols, window, columns = shape

    def ready():
        for copy in copies:
            copy.wait()

    slot_steps(window, first, member, cols, columns, dict(
        io=io, scratch=scratch, tile_rows=rows, ready=ready))


def inside_kernel(
    shape, offs, counts, amplitude, forward, inverse, probe, tile_in, part, probe_sum,
    ext, acc, pacc, *scratch_sems,
):
    *scratch, sems = scratch_sems
    rows, cols, window, columns = shape
    tiles = cols // LANE
    copies = run_copies([
        pltpu.make_async_copy(tile_in.at[:, :, span(k)], ext.at[:, k], sems.at[k])
        for k in range(tiles)
    ])
    acc[...] = jnp.zeros_like(acc)
    pacc[...] = jnp.zeros_like(pacc)
    slots_of(
        shape, 0, lambda row, tile: (row <= rows - window) & (tile < tiles - 2),
        (offs, counts, amplitude, forward, inverse, probe, ext, acc, pacc), scratch, copies)
    out = run_copies([
        pltpu.make_async_copy(acc, part, sems.at[0]),
        pltpu.make_async_copy(pacc, probe_sum, sems.at[1]),
    ])
    for copy in out:
        copy.wait()


def below_kernel(
    shape, offs, counts, amplitude, forward, inverse, probe, tile_in, lower_in, part, probe_in,
    own, strip, spill, probe_sum,
    ext, acc, pacc, *scratch_sems,
):
    *scratch, sems = scratch_sems
    rows, cols, window, columns = shape
    tiles = cols // LANE
    copies = [
        pltpu.make_async_copy(part, acc.at[:, :, pl.ds(0, rows), :], sems.at[2 * tiles]),
        pltpu.make_async_copy(probe_in, pacc, sems.at[2 * tiles + 1]),
    ]
    for k in range(tiles):
        copies.append(pltpu.make_async_copy(
            tile_in.at[:, :, span(k)], ext.at[:, k, pl.ds(0, rows), :], sems.at[2 * k]))
        copies.append(pltpu.make_async_copy(
            lower_in.at[:, :, span(k)], ext.at[:, k, pl.ds(rows, window), :], sems.at[2 * k + 1]))
    run_copies(copies)
    acc[:, :, rows:, :] = jnp.zeros((2, tiles, window, LANE), F32)
    slots_of(
        shape, 0, lambda row, tile: (row > rows - window) & (tile < tiles - 2),
        (offs, counts, amplitude, forward, inverse, probe, ext, acc, pacc), scratch, copies)
    out = []
    for k in range(tiles - 2):
        out.append(pltpu.make_async_copy(
            acc.at[:, k, pl.ds(0, rows), :], own.at[:, :, span(k)], sems.at[2 * k]))
        out.append(pltpu.make_async_copy(
            acc.at[:, k, pl.ds(rows, window), :], strip.at[:, :, span(k)], sems.at[2 * k + 1]))
    out.append(pltpu.make_async_copy(acc.at[:, pl.ds(tiles - 2, 2)], spill, sems.at[2 * tiles]))
    out.append(pltpu.make_async_copy(pacc, probe_sum, sems.at[2 * tiles + 1]))
    run_copies(out)
    for copy in out:
        copy.wait()


def across_kernel(
    shape, offs, counts, amplitude, forward, inverse, probe, tile_in, lower_in, top_in, bottom_in, corner_in,
    spill, probe_in, own_in, strip_in,
    own, strip, top, bottom, corner, probe_sum,
    ext, acc, pacc, *scratch_sems,
):
    *scratch, sems = scratch_sems
    rows, cols, window, columns = shape
    first = cols // LANE - 2
    copies = [
        pltpu.make_async_copy(spill, acc.at[:, pl.ds(0, 2)], sems.at[0]),
        pltpu.make_async_copy(probe_in, pacc, sems.at[1]),
    ]
    for k in range(2):
        for n, (source, start, count) in enumerate((
            (tile_in.at[:, :, span(first + k)], 0, rows),
            (lower_in.at[:, :, span(first + k)], rows, window),
        )):
            copies.append(pltpu.make_async_copy(
                source, ext.at[:, k, pl.ds(start, count), :], sems.at[2 + 5 * k + n]))
        for n, (source, start, count) in enumerate((
            (top_in, 0, window), (bottom_in, window, rows - window), (corner_in, rows, window),
        )):
            copies.append(pltpu.make_async_copy(
                source.at[:, :, span(k)], ext.at[:, 2 + k, pl.ds(start, count), :], sems.at[4 + 5 * k + n]))
    run_copies(copies)
    acc[:, 2:] = jnp.zeros_like(acc[:, 2:])
    slots_of(
        shape, first, lambda row, tile: tile >= first,
        (offs, counts, amplitude, forward, inverse, probe, ext, acc, pacc), scratch, copies)
    out = [pltpu.make_async_copy(pacc, probe_sum, sems.at[0])]
    for k in range(2):
        for n, (target, place, start, count) in enumerate((
            (own.at[:, :, span(first + k)], k, 0, rows),
            (strip.at[:, :, span(first + k)], k, rows, window),
            (top.at[:, :, span(k)], 2 + k, 0, window),
            (bottom.at[:, :, span(k)], 2 + k, window, rows - window),
            (corner.at[:, :, span(k)], 2 + k, rows, window),
        )):
            out.append(pltpu.make_async_copy(
                acc.at[:, place, pl.ds(start, count), :], target, sems.at[1 + 5 * k + n]))
    run_copies(out)
    for copy in out:
        copy.wait()


def exchange_total(value, axis):
    count = lax.axis_size(axis)
    step = 1
    while step < count:
        masks = (1, 2, 3) if 4 * step <= count else (1,)
        terms = [value] + [
            lax.ppermute(value, axis, [(k, k ^ (mask * step)) for k in range(count)]) for mask in masks
        ]
        while len(terms) > 1:
            terms = [terms[k] + terms[k + 1] for k in range(0, len(terms), 2)]
        value = terms[0]
        step *= len(masks) + 1
    return value


def per_device(object_field, illumination, amplitude, offsets, slot_counts):
    rows, cols = object_field.shape[1:]
    window = illumination.shape[1]
    slots = offsets.shape[0]
    columns = lax.axis_size("col")
    shape = (rows, cols, window, columns)
    tiles = cols // LANE
    reach = rows + window
    forward, inverse = dft_blocks(window)
    forward, inverse = jnp.asarray(forward), jnp.asarray(inverse)
    params = pltpu.CompilerParams(vmem_limit_bytes=VMEM_LIMIT)

    def sds(*dims):
        return jax.ShapeDtypeStruct(dims, F32)

    def slots_call(kernel, count, outs, extra, place, tiles_held, aliases=None):
        return pl.pallas_call(
            functools.partial(kernel, shape),
            out_shape=[sds(*dims) for dims in outs],
            in_specs=[SMEM, SMEM] + [HBM] * (4 + len(extra)),
            out_specs=[HBM] * len(outs),
            input_output_aliases=aliases or {},
            scratch_shapes=make_scratch(window, tiles_held, place, 12),
            compiler_params=params,
            cost_estimate=pl.CostEstimate(
                flops=32 * window**3 * count, bytes_accessed=2**20 * count, transcendentals=0),
            name=kernel.__name__,
        )(offsets, slot_counts, amplitude, forward, inverse, illumination, *extra)

    plane = (2, window, window)
    (top_own,) = slices(object_field, ((0, window, 0, window),), "slice_top")
    tile, top_own = lax.optimization_barrier((object_field, top_own))
    bottom_own, lower_own = slices(
        tile, ((window, rows - window, 0, window), (0, window, 0, cols)), "slice_rest")
    top_right = shifted(top_own, "col", -1)
    lower = shifted(lower_own, "row", -1)
    bottom_right = shifted(bottom_own, "col", -1)
    part, probe_sum = slots_call(
        inside_kernel, 0, [(2, tiles, rows, LANE), plane], (object_field,), rows, tiles)
    top_right, part = lax.optimization_barrier((top_right, part))
    corner_right = shifted(top_right, "row", -1)
    own, strip, spill, probe_sum = slots_call(
        below_kernel, 8, [(2, rows, cols), (2, window, cols), (2, 2, reach, LANE), plane],
        (object_field, lower, part, probe_sum), reach, tiles)
    own, strip, top, bottom, corner, probe_sum = slots_call(
        across_kernel, 8,
        [(2, rows, cols), (2, window, cols), plane, (2, rows - window, window), plane, plane],
        (object_field, lower, top_right, bottom_right, corner_right, spill, probe_sum, own, strip),
        reach, 4, {13: 0, 14: 1})

    corner_back = shifted(corner, "row", 1)
    bottom_back = shifted(bottom, "col", 1)
    pieces = lax.axis_size("row")
    scattered = lax.all_to_all(
        probe_sum.reshape(pieces, -1, window), "row", 0, 0, tiled=True)
    scattered, corner_back, bottom_back, strip = lax.optimization_barrier(
        (scattered, corner_back, bottom_back, strip))
    top_back = shifted(top + corner_back, "col", 1)
    strip_back = shifted(strip, "row", 1)
    piece = exchange_total(jnp.sum(scattered, axis=0), "col")
    summed = lax.all_gather(piece, "row").reshape(plane)
    own = merge(own, (strip_back, bottom_back),
                ((0, window, 0, cols), (window, rows - window, 0, window)), "first_merge")
    own = merge(own, (top_back,), ((0, window, 0, window),), "last_merge")
    live_total = slots * lax.axis_size("row") * lax.axis_size("col") // 2
    return own, summed * (1.0 / math.sqrt(live_total))


def solution(mesh):
    return jax.shard_map(
        per_device,
        mesh=mesh,
        in_specs=(
            P(None, "row", "col"),
            P(),
            P(("row", "col"), None, None),
            P(("row", "col"), None),
            P(),
        ),
        out_specs=(P(None, "row", "col"), P()),
        check_vma=False,
    )
```

```python
import functools
import math

import jax
import jax.numpy as jnp
import numpy as np
from jax import lax
from jax.experimental import pallas as pl
from jax.experimental.pallas import tpu as pltpu
from jax.sharding import PartitionSpec as P

LANE = 128
CHUNK = 32
PAIR = 4
VMEM_LIMIT = 44 * 1024 * 1024
F32 = jnp.float32
BF16 = jnp.bfloat16


def shifted(value, axis, steps):
    count = lax.axis_size(axis)
    leading, last = (max(0, -steps), min(count, count - steps))
    return lax.ppermute(value, axis, [(source, source + steps) for source in range(leading, last)])


def dft_blocks(window):
    index = np.arange(window)
    angle = (index[:, None] * index[None, :] % window) * (2.0 * math.pi / window)
    cosine = np.cos(angle) / math.sqrt(window)
    sine = np.sin(angle) / math.sqrt(window)
    forward = np.block([[cosine, sine], [-sine, cosine]])
    inverse = np.block([[cosine, -sine], [sine, cosine]])
    return forward.astype(BF16), inverse.astype(BF16)


def slot_steps(window, first, member, tile_cols, columns, refs):
    (offs, counts, amplitude, *tables_in, ext, acc, pacc) = refs["io"]
    (chosen, amp, patch, ext_wave, half, resid, back_half, amp_sem, *tables, table_sem) = refs["scratch"]
    (forward, inverse, probe) = tables
    loads = run_copies([
        pltpu.make_async_copy(tables_in[k], tables[k], table_sem.at[k]) for k in range(3)])
    slots = offs.shape[0]
    live = counts[lax.axis_index("row") * columns + lax.axis_index("col")]
    tile_rows = refs["tile_rows"]

    def first_tile(col):
        return lax.div(jnp.maximum(col - 1, 0), LANE)

    def pick(j, n):
        tile = first_tile(lax.rem(offs[j, 1], tile_cols))
        chosen[n] = j
        take = (j < live) & member(lax.rem(offs[j, 0], tile_rows), tile)
        return n + take.astype(jnp.int32)

    total = lax.fori_loop(0, slots, pick, jnp.int32(0))

    def fetch(i):
        buffer = lax.rem(i, 2 * PAIR)
        return pltpu.make_async_copy(
            amplitude.at[chosen[i]], amp.at[buffer], amp_sem.at[buffer])

    whole = lax.div(total, PAIR)
    left_over = total - whole * PAIR
    half_group = (left_over > 0) & (left_over <= PAIR // 2)
    full_groups = whole + (left_over > PAIR // 2).astype(jnp.int32)
    padded = full_groups * PAIR + half_group.astype(jnp.int32) * (PAIR // 2)

    for k in range(PAIR - 1):
        @pl.when(total > 0)
        def _():
            chosen[total + k] = chosen[total - 1]

    def fetch_from(base):
        for k in range(PAIR):
            @pl.when(base + k < padded)
            def _():
                fetch(base + k).start()

    fetch_from(0)

    refs["ready"]()
    for load in loads:
        load.wait()
    lane = lax.broadcasted_iota(jnp.int32, (CHUNK, LANE), 1)

    def body(base, size):
        fetch_from(base + size)
        places = []
        for s in range(size):
            j = chosen[base + s]
            row = lax.rem(offs[j, 0], tile_rows)
            col = lax.rem(offs[j, 1], tile_cols)
            tile = first_tile(col)
            places.append((row, tile - first, col - tile * LANE))
        def extract(s):
            row, tile, rest = places[s]
            turn = lax.rem(LANE - rest, LANE)
            head = lane < LANE - rest
            for line in range(0, window, CHUNK):
                rows = pl.ds(row + line, CHUNK)
                here = slice(line, line + CHUNK)
                planes = []
                for plane in range(2):
                    turned = [
                        pltpu.roll(ext[plane, tile + k, rows, :], turn, 1) for k in range(3)
                    ]
                    planes.append(
                        [jnp.where(head, turned[k], turned[k + 1]) for k in range(2)]
                    )
                for k in range(2):
                    cols = slice(k * LANE, (k + 1) * LANE)
                    real, imag = planes[0][k], planes[1][k]
                    patch[s, 0, here, cols] = real
                    patch[s, 1, here, cols] = imag
                    probe_real, probe_imag = probe[0, here, cols], probe[1, here, cols]
                    ext_wave[s, line : line + CHUNK, cols] = (
                        probe_real * real - probe_imag * imag
                    ).astype(BF16)
                    ext_wave[s, window + line : window + line + CHUNK, cols] = (
                        probe_real * imag + probe_imag * real
                    ).astype(BF16)
                yield

        def rows_forward(s):
            for n in range(2):
                part = slice(n * window, (n + 1) * window)
                half[s, :, part] = jnp.dot(
                    forward[part, :], ext_wave[s], preferred_element_type=F32).astype(BF16)
                yield

        def columns_forward(s):
            far = jnp.dot(half[s], inverse[...], preferred_element_type=F32)
            yield
            buffer = lax.rem(base + s, 2 * PAIR)
            for line in range(0, window, CHUNK):
                here = slice(line, line + CHUNK)
                real, imag = far[here, :window], far[here, window:]
                level = amp[buffer, here, :].astype(F32)
                factor = 1.0 - level * lax.rsqrt(real * real + imag * imag + 0.25)
                resid[s, here, :] = (real * factor).astype(BF16)
                resid[s, window + line : window + line + CHUNK, :] = (imag * factor).astype(BF16)
                yield

        def rows_back(s):
            for n in range(2):
                part = slice(n * window, (n + 1) * window)
                back_half[s, :, part] = jnp.dot(
                    inverse[part, :], resid[s], preferred_element_type=F32).astype(BF16)
                yield

        def columns_back(s):
            row, tile, rest = places[s]
            back = jnp.dot(back_half[s], forward[...], preferred_element_type=F32)
            yield
            turn = lax.rem(rest, LANE)
            tail = lane >= rest
            weight = (base + s < total).astype(F32)
            for line in range(0, window, CHUNK):
                rows = pl.ds(row + line, CHUNK)
                here = slice(line, line + CHUNK)
                terms = [[], []]
                for k in range(2):
                    cols = slice(k * LANE, (k + 1) * LANE)
                    real = back[here, k * LANE : (k + 1) * LANE]
                    imag = back[here, window + k * LANE : window + (k + 1) * LANE]
                    if s == size - 1:
                        real, imag = real * weight, imag * weight
                    probe_real, probe_imag = probe[0, here, cols], probe[1, here, cols]
                    patch_real, patch_imag = patch[s, 0, here, cols], patch[s, 1, here, cols]
                    pacc[0, here, cols] += patch_real * real + patch_imag * imag
                    pacc[1, here, cols] += patch_real * imag - patch_imag * real
                    terms[0].append(pltpu.roll(probe_real * real + probe_imag * imag, turn, 1))
                    terms[1].append(pltpu.roll(probe_real * imag - probe_imag * real, turn, 1))
                for plane in range(2):
                    left, right = terms[plane]
                    acc[plane, tile, rows, :] += jnp.where(tail, left, 0.0)
                    acc[plane, tile + 1, rows, :] += jnp.where(tail, right, left)
                    acc[plane, tile + 2, rows, :] += jnp.where(tail, 0.0, right)
                yield

        for s in range(size):
            fetch(base + s).wait()
        stages = (extract, rows_forward, columns_forward, rows_back, columns_back)
        for step in range(size + len(stages) - 1):
            running = [
                stages[step - s](s) for s in reversed(range(size)) if 0 <= step - s < len(stages)]
            for work in running:
                for _ in work:
                    pass

    def full(group, carry):
        body(group * PAIR, PAIR)
        return carry

    lax.fori_loop(0, full_groups, full, 0)

    @pl.when(half_group)
    def _():
        body(full_groups * PAIR, PAIR // 2)


def run_copies(copies):
    for copy in copies:
        copy.start()
    return copies


def make_scratch(window, tiles, rows, copies):
    return [
        pltpu.VMEM((2, tiles, rows, LANE), F32),
        pltpu.VMEM((2, tiles, rows, LANE), F32),
        pltpu.VMEM((2, window, window), F32),
        pltpu.SMEM((32,), jnp.int32),
        pltpu.VMEM((2 * PAIR, window, window), BF16),
        pltpu.VMEM((PAIR, 2, window, window), F32),
        pltpu.VMEM((PAIR, 2 * window, window), BF16),
        pltpu.VMEM((PAIR, window, 2 * window), BF16),
        pltpu.VMEM((PAIR, 2 * window, window), BF16),
        pltpu.VMEM((PAIR, window, 2 * window), BF16),
        pltpu.SemaphoreType.DMA((2 * PAIR,)),
        pltpu.VMEM((2 * window, 2 * window), BF16),
        pltpu.VMEM((2 * window, 2 * window), BF16),
        pltpu.VMEM((2, window, window), F32),
        pltpu.SemaphoreType.DMA((3,)),
        pltpu.SemaphoreType.DMA((copies,)),
    ]


SMEM = pl.BlockSpec(memory_space=pltpu.SMEM)
VMEM = pl.BlockSpec(memory_space=pltpu.VMEM)
HBM = pl.BlockSpec(memory_space=pl.ANY)


def span(tile, count=1):
    return pl.ds(tile * LANE, count * LANE)


def slice_kernel(spots, tile_in, *refs):
    *outs, sems = refs
    copies = run_copies([
        pltpu.make_async_copy(
            tile_in.at[:, pl.ds(row, rows), pl.ds(col, cols)], outs[k], sems.at[k])
        for k, (row, rows, col, cols) in enumerate(spots)
    ])
    for copy in copies:
        copy.wait()


def slices(tile, spots, name):
    return pl.pallas_call(
        functools.partial(slice_kernel, spots),
        out_shape=[jax.ShapeDtypeStruct((2, rows, cols), F32) for _, rows, _, cols in spots],
        in_specs=[HBM],
        out_specs=[VMEM] * len(spots),
        scratch_shapes=[pltpu.SemaphoreType.DMA((len(spots),))],
        name=name,
    )(tile)


def merge_kernel(places, own_in, *refs):
    count = len(places)
    added, (own, *held), sems = refs[:count], refs[count:-1], refs[-1]
    spots = [
        own.at[:, pl.ds(row, rows), pl.ds(col, cols)] for row, rows, col, cols in places]
    loads = []
    for k in range(count):
        loads += run_copies([
            pltpu.make_async_copy(spots[k], held[2 * k], sems.at[3 * k]),
            pltpu.make_async_copy(added[k], held[2 * k + 1], sems.at[3 * k + 1]),
        ])
    stores = []
    for k in range(count):
        loads[2 * k].wait()
        loads[2 * k + 1].wait()
        held[2 * k][...] += held[2 * k + 1][...]
        stores += run_copies([pltpu.make_async_copy(held[2 * k], spots[k], sems.at[3 * k + 2])])
    for store in stores:
        store.wait()


def merge(own, blocks, places, name):
    scratch = []
    for _, rows, _, cols in places:
        scratch += [pltpu.VMEM((2, rows, cols), F32)] * 2
    return pl.pallas_call(
        functools.partial(merge_kernel, places),
        out_shape=jax.ShapeDtypeStruct(own.shape, F32),
        in_specs=[HBM] * (1 + len(blocks)),
        out_specs=HBM,
        input_output_aliases={0: 0},
        scratch_shapes=scratch + [pltpu.SemaphoreType.DMA((3 * len(blocks),))],
        compiler_params=pltpu.CompilerParams(vmem_limit_bytes=VMEM_LIMIT),
        name=name,
    )(own, *blocks)


def slots_of(shape, first, member, io, scratch, copies):
    rows, cols, window, columns = shape

    def ready():
        for copy in copies:
            copy.wait()

    slot_steps(window, first, member, cols, columns, dict(
        io=io, scratch=scratch, tile_rows=rows, ready=ready))


def inside_kernel(
    shape, offs, counts, amplitude, forward, inverse, probe, tile_in, part, probe_sum,
    ext, acc, pacc, *scratch_sems,
):
    *scratch, sems = scratch_sems
    rows, cols, window, columns = shape
    tiles = cols // LANE
    copies = run_copies([
        pltpu.make_async_copy(tile_in.at[:, :, span(k)], ext.at[:, k], sems.at[k])
        for k in range(tiles)
    ])
    acc[...] = jnp.zeros_like(acc)
    pacc[...] = jnp.zeros_like(pacc)
    slots_of(
        shape, 0, lambda row, tile: (row <= rows - window) & (tile < tiles - 2),
        (offs, counts, amplitude, forward, inverse, probe, ext, acc, pacc), scratch, copies)
    out = run_copies([
        pltpu.make_async_copy(acc, part, sems.at[0]),
        pltpu.make_async_copy(pacc, probe_sum, sems.at[1]),
    ])
    for copy in out:
        copy.wait()


def below_kernel(
    shape, offs, counts, amplitude, forward, inverse, probe, tile_in, lower_in, part, probe_in,
    own, strip, spill, probe_sum,
    ext, acc, pacc, *scratch_sems,
):
    *scratch, sems = scratch_sems
    rows, cols, window, columns = shape
    tiles = cols // LANE
    copies = [
        pltpu.make_async_copy(part, acc.at[:, :, pl.ds(0, rows), :], sems.at[2 * tiles]),
        pltpu.make_async_copy(probe_in, pacc, sems.at[2 * tiles + 1]),
    ]
    for k in range(tiles):
        copies.append(pltpu.make_async_copy(
            tile_in.at[:, :, span(k)], ext.at[:, k, pl.ds(0, rows), :], sems.at[2 * k]))
        copies.append(pltpu.make_async_copy(
            lower_in.at[:, :, span(k)], ext.at[:, k, pl.ds(rows, window), :], sems.at[2 * k + 1]))
    run_copies(copies)
    acc[:, :, rows:, :] = jnp.zeros((2, tiles, window, LANE), F32)
    slots_of(
        shape, 0, lambda row, tile: (row > rows - window) & (tile < tiles - 2),
        (offs, counts, amplitude, forward, inverse, probe, ext, acc, pacc), scratch, copies)
    out = []
    for k in range(tiles - 2):
        out.append(pltpu.make_async_copy(
            acc.at[:, k, pl.ds(0, rows), :], own.at[:, :, span(k)], sems.at[2 * k]))
        out.append(pltpu.make_async_copy(
            acc.at[:, k, pl.ds(rows, window), :], strip.at[:, :, span(k)], sems.at[2 * k + 1]))
    out.append(pltpu.make_async_copy(acc.at[:, pl.ds(tiles - 2, 2)], spill, sems.at[2 * tiles]))
    out.append(pltpu.make_async_copy(pacc, probe_sum, sems.at[2 * tiles + 1]))
    run_copies(out)
    for copy in out:
        copy.wait()


def across_kernel(
    shape, offs, counts, amplitude, forward, inverse, probe, tile_in, lower_in, top_in, bottom_in, corner_in,
    spill, probe_in, own_in, strip_in,
    own, strip, top, bottom, corner, probe_sum,
    ext, acc, pacc, *scratch_sems,
):
    *scratch, sems = scratch_sems
    rows, cols, window, columns = shape
    first = cols // LANE - 2
    copies = [
        pltpu.make_async_copy(spill, acc.at[:, pl.ds(0, 2)], sems.at[0]),
        pltpu.make_async_copy(probe_in, pacc, sems.at[1]),
    ]
    for k in range(2):
        for n, (source, start, count) in enumerate((
            (tile_in.at[:, :, span(first + k)], 0, rows),
            (lower_in.at[:, :, span(first + k)], rows, window),
        )):
            copies.append(pltpu.make_async_copy(
                source, ext.at[:, k, pl.ds(start, count), :], sems.at[2 + 5 * k + n]))
        for n, (source, start, count) in enumerate((
            (top_in, 0, window), (bottom_in, window, rows - window), (corner_in, rows, window),
        )):
            copies.append(pltpu.make_async_copy(
                source.at[:, :, span(k)], ext.at[:, 2 + k, pl.ds(start, count), :], sems.at[4 + 5 * k + n]))
    run_copies(copies)
    acc[:, 2:] = jnp.zeros_like(acc[:, 2:])
    slots_of(
        shape, first, lambda row, tile: tile >= first,
        (offs, counts, amplitude, forward, inverse, probe, ext, acc, pacc), scratch, copies)
    out = [pltpu.make_async_copy(pacc, probe_sum, sems.at[0])]
    for k in range(2):
        for n, (target, place, start, count) in enumerate((
            (own.at[:, :, span(first + k)], k, 0, rows),
            (strip.at[:, :, span(first + k)], k, rows, window),
            (top.at[:, :, span(k)], 2 + k, 0, window),
            (bottom.at[:, :, span(k)], 2 + k, window, rows - window),
            (corner.at[:, :, span(k)], 2 + k, rows, window),
        )):
            out.append(pltpu.make_async_copy(
                acc.at[:, place, pl.ds(start, count), :], target, sems.at[1 + 5 * k + n]))
    run_copies(out)
    for copy in out:
        copy.wait()


def exchange_total(value, axis):
    count = lax.axis_size(axis)
    step = 1
    while step < count:
        masks = (1, 2, 3) if 4 * step <= count else (1,)
        terms = [value] + [
            lax.ppermute(value, axis, [(k, k ^ (mask * step)) for k in range(count)]) for mask in masks
        ]
        while len(terms) > 1:
            terms = [terms[k] + terms[k + 1] for k in range(0, len(terms), 2)]
        value = terms[0]
        step *= len(masks) + 1
    return value


def per_device(object_field, illumination, amplitude, offsets, slot_counts):
    rows, cols = object_field.shape[1:]
    window = illumination.shape[1]
    slots = offsets.shape[0]
    columns = lax.axis_size("col")
    shape = (rows, cols, window, columns)
    tiles = cols // LANE
    reach = rows + window
    forward, inverse = dft_blocks(window)
    forward, inverse = jnp.asarray(forward), jnp.asarray(inverse)
    params = pltpu.CompilerParams(vmem_limit_bytes=VMEM_LIMIT)

    def sds(*dims):
        return jax.ShapeDtypeStruct(dims, F32)

    def slots_call(kernel, count, outs, extra, place, tiles_held, aliases=None):
        return pl.pallas_call(
            functools.partial(kernel, shape),
            out_shape=[sds(*dims) for dims in outs],
            in_specs=[SMEM, SMEM] + [HBM] * (4 + len(extra)),
            out_specs=[HBM] * len(outs),
            input_output_aliases=aliases or {},
            scratch_shapes=make_scratch(window, tiles_held, place, 12),
            compiler_params=params,
            cost_estimate=pl.CostEstimate(
                flops=32 * window**3 * count, bytes_accessed=2**20 * count, transcendentals=0),
            name=kernel.__name__,
        )(offsets, slot_counts, amplitude, forward, inverse, illumination, *extra)

    plane = (2, window, window)
    top_own, bottom_own, lower_own = slices(
        object_field,
        ((0, window, 0, window), (window, rows - window, 0, window), (0, window, 0, cols)),
        "slice_tile")
    top_right = shifted(top_own, "col", -1)
    lower = shifted(lower_own, "row", -1)
    bottom_right = shifted(bottom_own, "col", -1)
    part, probe_sum = slots_call(
        inside_kernel, 0, [(2, tiles, rows, LANE), plane], (object_field,), rows, tiles)
    top_right, part = lax.optimization_barrier((top_right, part))
    corner_right = shifted(top_right, "row", -1)
    own, strip, spill, probe_sum = slots_call(
        below_kernel, 8, [(2, rows, cols), (2, window, cols), (2, 2, reach, LANE), plane],
        (object_field, lower, part, probe_sum), reach, tiles)
    own, strip, top, bottom, corner, probe_sum = slots_call(
        across_kernel, 8,
        [(2, rows, cols), (2, window, cols), plane, (2, rows - window, window), plane, plane],
        (object_field, lower, top_right, bottom_right, corner_right, spill, probe_sum, own, strip),
        reach, 4, {13: 0, 14: 1})

    corner_back = shifted(corner, "row", 1)
    bottom_back = shifted(bottom, "col", 1)
    pieces = lax.axis_size("row")
    scattered = lax.all_to_all(
        probe_sum.reshape(pieces, -1, window), "row", 0, 0, tiled=True)
    scattered, corner_back, bottom_back, strip = lax.optimization_barrier(
        (scattered, corner_back, bottom_back, strip))
    top_back = shifted(top + corner_back, "col", 1)
    strip_back = shifted(strip, "row", 1)
    piece = exchange_total(jnp.sum(scattered, axis=0), "col")
    summed = lax.all_gather(piece, "row").reshape(plane)
    own = merge(own, (strip_back, bottom_back),
                ((0, window, 0, cols), (window, rows - window, 0, window)), "first_merge")
    own = merge(own, (top_back,), ((0, window, 0, window),), "last_merge")
    live_total = slots * lax.axis_size("row") * lax.axis_size("col") // 2
    return own, summed * (1.0 / math.sqrt(live_total))


def solution(mesh):
    return jax.shard_map(
        per_device,
        mesh=mesh,
        in_specs=(
            P(None, "row", "col"),
            P(),
            P(("row", "col"), None, None),
            P(("row", "col"), None),
            P(),
        ),
        out_specs=(P(None, "row", "col"), P()),
        check_vma=False,
    )
```
